32 devices in a mesh: groups: 2 (over x), fsdp: 16 (over z, y, core).
Axes of the slice: x: 2, y: 2, z: 4, core: 2. Of those that a mesh axis runs over, the one named last changes fastest.
Arguments:
- hidden_in: bfloat16 [2, 32, 8192], P(None, 'groups', 'fsdp'), parts along dimension 1, may hold values from -6 to 6
- norm_gain: bfloat16 [8192], P('fsdp'), may hold values from 0.099609375 to 1.8984375
- w_query: bfloat16 [8192, 8192], P(None, 'fsdp'), may hold values from -0.0625 to 0.0625
- w_keyval: bfloat16 [8192, 2048], P('fsdp'), may hold values from -0.0625 to 0.0625
- w_out: bfloat16 [8192, 8192], P('fsdp'), may hold values from -0.75 to 0.75
- q_delta: bfloat16 [1536, 128, 128], P(('groups', 'fsdp')), parts along dimension 0, may hold values from -0.125 to 0.125
- q_rows: int32 [1536], P(('groups', 'fsdp')), parts along dimension 0, may hold values from 0 to 63, as said below
- q_cols: int32 [1536], P(('groups', 'fsdp')), parts along dimension 0, may hold values from 0 to 63
- q_count: int32 [32], P(('groups', 'fsdp')), parts along dimension 0, may hold values from 1 to 48, as said below
- o_delta: bfloat16 [1536, 128, 128], P(('groups', 'fsdp')), parts along dimension 0, may hold values from -1 to 1
- o_rows: int32 [1536], P(('groups', 'fsdp')), parts along dimension 0, may hold values from 0 to 63, as said below
- o_cols: int32 [1536], P(('groups', 'fsdp')), parts along dimension 0, may hold values from 0 to 63, as said below
- o_count: int32 [32], P(('groups', 'fsdp')), parts along dimension 0, may hold values from 1 to 48, as said below
- key_cache: bfloat16 [32, 8192, 128], P('groups', 'fsdp'), parts along dimension 0, may hold values from -500 to 500
- value_cache: bfloat16 [32, 8192, 128], P('groups', 'fsdp'), parts along dimension 0, may hold values from -6 to 6
- lengths: int32 [32], P('groups'), parts along dimension 0, may hold values from 1 to 1024, as said below
Outputs:
- attended: bfloat16 [2, 32, 8192], P(None, 'groups', 'fsdp'), parts along dimension 1
The draws below stay inside these ranges and needn't reach their ends.
There are 2 independent parts, one for each index of `groups`. The reference program is written for one: setup_inputs(seed, part) draws one part's arguments, and reference() takes and returns one part's arrays. A program takes and returns all parts, laid end to end along the dimension named above; an argument that names none is the same for every part. Nothing has to cross between parts.
Inputs may be any that keep to these rules, and one draw needn't show every extreme that they name: `q_rows`: slots of owner o name row blocks of that owner's rows o*8192/(128*16) to (o+1)*8192/(128*16)-1; the (row, column) pairs of one owner's slots are distinct. `q_count`: only the first count slots of an owner are live; some owner has 48. `o_rows`: the (row, column) pairs of one owner's slots are distinct. `o_cols`: slots of owner o name column blocks of that owner's columns o*8192/(128*16) to (o+1)*8192/(128*16)-1. `o_count`: only the first count slots of an owner are live; some owner has 48. `lengths`: some sequence has 1024.
All inputs are finite; a program needn't handle non-finite values.
Results may differ from the reference program's by a relative error of at most 0.012.
The reference program's roundings to bfloat16 on the way count: a program that leaves them out, or rounds other values in their place, can miss the bound.
Values may be sent and summed in bfloat16 or wider, within the bound.
A program may use at most 128 MiB of HBM per device.

```python
import jax
import jax.numpy as jnp
from jax import lax

D = 8192
HEADS = 64
KVH = 8
HD = 128
BLOCK = 128
STEPS = 2
SEQS = 16
CAP = 48
CACHE = 1024
SLOTS = 768
N_FSDP = 16


def block_layout(key, salt):
    key = jax.random.fold_in(key, salt)
    keys = jax.random.split(key, N_FSDP)
    across = HEADS * HD // BLOCK
    own_rows = D // BLOCK // N_FSDP
    picks = jax.vmap(lambda k: jax.random.permutation(k, own_rows * across)[:CAP])(keys)
    local = picks // across
    other = picks % across
    owner = jnp.arange(N_FSDP, dtype=jnp.int32)[:, None]
    own = owner * own_rows + local
    return (own.reshape(-1).astype(jnp.int32), other.reshape(-1).astype(jnp.int32))


def skewed_counts(key):
    first, second = jax.random.split(key)
    drawn = jax.random.randint(first, (N_FSDP,), 0, CAP)
    counts = 1 + drawn * drawn // CAP
    full = jax.random.randint(second, (), 0, N_FSDP)
    return jnp.where(jnp.arange(N_FSDP) == full, CAP, counts).astype(jnp.int32)


def draw_q_rows(key, part):
    return block_layout(key, 11)[0]


def draw_q_cols(key, part):
    return block_layout(key, 11)[1]


def draw_o_rows(key, part):
    return block_layout(key, 12)[1]


def draw_o_cols(key, part):
    return block_layout(key, 12)[0]


def draw_q_count(key, part):
    key = jax.random.fold_in(key, 21)
    return skewed_counts(key)


def draw_o_count(key, part):
    key = jax.random.fold_in(key, 22)
    return skewed_counts(key)


def draw_lengths(key, part):
    key = jax.random.fold_in(key, 31)
    first, second = jax.random.split(key)
    drawn = jax.random.randint(first, (SEQS,), 1, CACHE + 1)
    full = jax.random.randint(second, (), 0, SEQS)
    return jnp.where(jnp.arange(SEQS) == full, CACHE, drawn).astype(jnp.int32)


def draw_key_cache(key, part):
    key = jax.random.fold_in(key, 41)
    first = jax.random.fold_in(key, 0)
    shape = (SEQS, KVH * CACHE, HD)
    entries = jnp.clip(jax.random.normal(first, shape, jnp.float32), -6.0, 6.0)
    return entries.astype(jnp.bfloat16)


def raised(result, own_key, source, target, shards_of, factor):
    def block_of(dim):
        return (jnp.arange(result.shape[dim]) // (result.shape[dim] // shards_of)).reshape((-1,) + (1,) * (result.ndim - 1 - dim))

    first = jax.random.permutation(own_key, shards_of)[block_of(target)]
    far = (block_of(target) + shards_of // 2) % shards_of
    return jnp.where((block_of(source) == first) | (block_of(source) == far), factor * result, result)


def block_scale(own_key, dims, cuts, least, high):
    gain, own = 1.0, jax.random.fold_in(own_key, 6)
    for dim, shards_of in cuts:
        steps = jnp.exp(jax.random.uniform(jax.random.fold_in(own, dim), (shards_of,), jnp.float32, least / len(cuts), high / len(cuts)))
        gain = gain * jnp.repeat(steps, dims[dim] // shards_of).reshape([-1 if axis == dim else 1 for axis in range(len(dims))])
    return gain


def normal_values(rng, extent, scale, bound, cuts=(), held_as=jnp.bfloat16):
    entries = scale * jax.random.normal(rng, extent, jnp.float32)
    if cuts:
        entries = entries * block_scale(rng, extent, cuts, -0.22, 0.18)
    return jnp.clip(entries, -bound, bound).astype(held_as)


def noise_with(own_key, extent, spread, reach, cuts, heavy, kind=jnp.bfloat16):
    array = spread * jax.random.normal(own_key, extent, jnp.float32)
    if cuts:
        array = array * block_scale(own_key, extent, cuts, -0.22, 0.18)
    return jnp.clip(raised(array, jax.random.fold_in(own_key, 3), *heavy), -reach, reach).astype(kind)


def setup_inputs(seed: int = 0, part: int = 0) -> dict:
    streams_of = jax.random.split(jax.random.key(seed), 17)
    part_keys = jax.random.split(jax.random.fold_in(streams_of[16], part), 17)
    return {
        "hidden_in": normal_values(part_keys[0], (STEPS, SEQS, D), 1.0, 6.0, ((2, 16),)),
        "norm_gain": jnp.clip(1.0 + 0.18 * jax.random.normal(streams_of[1], (D,), jnp.float32), 0.099609375, 1.8984375).astype(jnp.bfloat16),
        "w_query": normal_values(streams_of[2], (D, HEADS * HD), D ** -0.5, 0.0625, ((1, 16),)),
        "w_keyval": normal_values(streams_of[3], (D, 2 * KVH * HD), D ** -0.5, 0.0625, ((0, 16),)),
        "w_out": noise_with(streams_of[4], (HEADS * HD, D), HD ** -0.5, 0.75, ((0, 16),), (0, 1, 16, 2.0)),
        "q_delta": normal_values(part_keys[5], (SLOTS, BLOCK, BLOCK), (D // 4) ** -0.5, 0.125, ((0, 16),)),
        "q_rows": draw_q_rows(jax.random.fold_in(jax.random.fold_in(streams_of[16], part), 71), part),
        "q_cols": draw_q_cols(jax.random.fold_in(jax.random.fold_in(streams_of[16], part), 71), part),
        "q_count": draw_q_count(jax.random.fold_in(jax.random.fold_in(streams_of[16], part), 71), part),
        "o_delta": normal_values(part_keys[9], (SLOTS, BLOCK, BLOCK), (HD // 4) ** -0.5, 1.0, ((0, 16),)),
        "o_rows": draw_o_rows(jax.random.fold_in(jax.random.fold_in(streams_of[16], part), 71), part),
        "o_cols": draw_o_cols(jax.random.fold_in(jax.random.fold_in(streams_of[16], part), 71), part),
        "o_count": draw_o_count(jax.random.fold_in(jax.random.fold_in(streams_of[16], part), 71), part),
        "key_cache": draw_key_cache(jax.random.fold_in(jax.random.fold_in(streams_of[16], part), 71), part),
        "value_cache": normal_values(part_keys[14], (SEQS, KVH * CACHE, HD), 1.0, 6.0, ((1, 16),)),
        "lengths": draw_lengths(jax.random.fold_in(jax.random.fold_in(streams_of[16], part), 71), part),
    }


theta_base = 1000000.0
eps = 1e-06
masked = -1e+30

def rotate(vec, position):
    half = vec.shape[-1] // 2
    freq = theta_base ** (-(jnp.arange(half, dtype=jnp.float32) * 2.0) / vec.shape[-1])
    angle = position[..., None] * freq
    cosine = jnp.cos(angle)
    sine = jnp.sin(angle)
    first = vec[..., :half]
    second = vec[..., half:]
    return jnp.concatenate([first * cosine - second * sine, second * cosine + first * sine], axis=-1)

def densify(values, rows, cols, counts, nrows, ncols):
    slots = values.shape[0]
    owners = counts.shape[0]
    cap = slots // owners
    alive = jnp.arange(slots, dtype=jnp.int32) % cap < jnp.repeat(counts, cap)
    kept = jnp.where(alive[:, None, None], values.astype(jnp.float32), 0.0)
    dense = jnp.zeros((nrows, ncols, values.shape[1], values.shape[2]), jnp.float32)
    dense = dense.at[rows, cols].add(kept)
    return dense.transpose(0, 2, 1, 3).reshape(nrows * values.shape[1], ncols * values.shape[2])

def reference(hidden_in, norm_gain, w_query, w_keyval, w_out, q_delta, q_rows, q_cols, q_count, o_delta, o_rows, o_cols, o_count, key_cache, value_cache, lengths):
    merged_q = (w_query.astype(jnp.float32) + densify(q_delta, q_rows, q_cols, q_count, D // BLOCK, HEADS * HD // BLOCK)).astype(jnp.bfloat16)
    merged_o = (w_out.astype(jnp.float32) + densify(o_delta, o_rows, o_cols, o_count, HEADS * HD // BLOCK, D // BLOCK)).astype(jnp.bfloat16)
    xf = hidden_in.astype(jnp.float32)
    power = lax.optimization_barrier(jnp.mean(xf * xf, axis=-1, keepdims=True))
    normed = (xf * lax.rsqrt(power + eps) * norm_gain.astype(jnp.float32)).astype(jnp.bfloat16)
    flat = normed.reshape(STEPS * SEQS, D)
    position = (lengths[None, :] + jnp.arange(STEPS, dtype=jnp.int32)[:, None]).astype(jnp.float32)
    query = jnp.dot(flat, merged_q, preferred_element_type=jnp.float32).reshape(STEPS, SEQS, HEADS, HD)
    query = rotate(query, position[:, :, None]).astype(jnp.bfloat16)
    keyval = jnp.dot(flat, w_keyval, preferred_element_type=jnp.float32).reshape(STEPS, SEQS, 2, KVH, HD)
    new_key = rotate(keyval[:, :, 0], position[:, :, None]).astype(jnp.bfloat16)
    new_value = keyval[:, :, 1].astype(jnp.bfloat16)
    keys_all = key_cache.reshape(SEQS, KVH, CACHE, HD)
    values_all = value_cache.reshape(SEQS, KVH, CACHE, HD)
    group = HEADS // KVH
    scale = HD ** (-0.5)
    valid_cache = (jnp.arange(CACHE, dtype=jnp.int32)[None, :] < lengths[:, None])[None, :, None, :]
    stepping = jnp.arange(STEPS, dtype=jnp.int32)
    valid_new = (stepping[None, :] <= stepping[:, None])[:, None, None, :]

    def one_group(index):
        cached_keys = lax.dynamic_index_in_dim(keys_all, index, 1, keepdims=False).astype(jnp.float32)
        cached_values = lax.dynamic_index_in_dim(values_all, index, 1, keepdims=False).astype(jnp.float32)
        grouped = lax.dynamic_slice_in_dim(query, index * group, group, 2).astype(jnp.float32)
        fresh_keys = lax.dynamic_index_in_dim(new_key, index, 2, keepdims=False).astype(jnp.float32)
        fresh_values = lax.dynamic_index_in_dim(new_value, index, 2, keepdims=False).astype(jnp.float32)
        cache_scores = jnp.einsum('tshd,scd->tshc', grouped, cached_keys) * scale
        new_scores = jnp.einsum('tshd,usd->tshu', grouped, fresh_keys) * scale
        cache_scores = jnp.where(valid_cache, cache_scores, masked)
        new_scores = jnp.where(valid_new, new_scores, masked)
        top = jnp.maximum(lax.optimization_barrier(jnp.max(cache_scores, -1)), lax.optimization_barrier(jnp.max(new_scores, -1)))
        cache_weights = jnp.where(valid_cache, jnp.exp(cache_scores - top[..., None]), 0.0)
        new_weights = jnp.where(valid_new, jnp.exp(new_scores - top[..., None]), 0.0)
        total = lax.optimization_barrier(jnp.sum(cache_weights, -1)) + lax.optimization_barrier(jnp.sum(new_weights, -1))
        cache_round = lax.optimization_barrier(cache_weights.astype(jnp.bfloat16)).astype(jnp.float32)
        new_round = lax.optimization_barrier(new_weights.astype(jnp.bfloat16)).astype(jnp.float32)
        mixed = jnp.einsum('tshc,scd->tshd', cache_round, cached_values) + jnp.einsum('tshu,usd->tshd', new_round, fresh_values)
        return (mixed / total[..., None]).astype(jnp.bfloat16)
    heads_out = lax.map(one_group, jnp.arange(KVH, dtype=jnp.int32))
    heads_out = heads_out.transpose(1, 2, 0, 3, 4).reshape(STEPS * SEQS, HEADS * HD)
    attended = jnp.dot(heads_out, merged_o, preferred_element_type=jnp.float32)
    return attended.astype(jnp.bfloat16).reshape(STEPS, SEQS, D)
```

```python
import functools

import jax
import jax.numpy as jnp
from jax import lax
from jax.experimental import pallas as pl
from jax.experimental.pallas import tpu as pltpu
from jax.sharding import PartitionSpec as P

HD = 128
BLOCK = 128
theta_base = 1000000.0
eps = 1e-06
masked = -1e30
MESH = pl.DeviceIdType.MESH
F32 = jnp.float32
BF16 = jnp.bfloat16
VM = pl.BlockSpec(memory_space=pltpu.VMEM)
SM = pl.BlockSpec(memory_space=pltpu.SMEM)
ANY = pl.BlockSpec(memory_space=pl.ANY)


def rcopy(src, dst, send, recv, device):
    return pltpu.make_async_remote_copy(
        src_ref=src, dst_ref=dst, send_sem=send, recv_sem=recv,
        device_id={"fsdp": device}, device_id_type=MESH,
    )


def greet(devices):
    barrier = pltpu.get_barrier_semaphore()
    for device in devices:
        pl.semaphore_signal(barrier, inc=1, device_id={"fsdp": device}, device_id_type=MESH)
    pl.semaphore_wait(barrier, len(devices))


def spread(n, me, buf, start, size, sems):
    chips = n // 2
    chip, core = me // 2, me % 2
    partner = me + 1 - 2 * core
    ss, sr, fs, fr = sems
    view = lambda dev: buf.at[pl.ds(dev * size, size)]
    out = []
    for d in range(1, chips):
        dst = 2 * ((chip + d) % chips) + core
        c = rcopy(view(me), view(me), ss.at[d], sr.at[d], dst)
        c.start()
        out.append(c)
    c = rcopy(view(me), view(me), fs.at[0], fr.at[0], partner)
    c.start()
    forwards = [c]
    return out, forwards


def pass_on(n, me, buf, size, sems, out, forwards):
    chips = n // 2
    chip, core = me // 2, me % 2
    partner = me + 1 - 2 * core
    ss, sr, fs, fr = sems
    for d in range(1, chips):
        out[d - 1].wait_recv()
        src = 2 * ((chip + chips - d) % chips) + core
        v = buf.at[pl.ds(src * size, size)]
        c = rcopy(v, v, fs.at[d], fr.at[d], partner)
        c.start()
        forwards.append(c)
    for c in forwards:
        c.wait_recv()
    for c in out + forwards:
        c.wait_send()


def rope(v, cosine, sine):
    return v * cosine + pltpu.roll(v, HD // 2, 1) * sine


def pack_kernel(
    cap, row_blocks, per, rows_ref, cols_ref, count_ref, delta_ref, pack_ref, place_ref, over_ref, seen_ref
):
    me = lax.axis_index("fsdp")
    n = place_ref.shape[0]
    pack_ref[...] = jnp.zeros_like(pack_ref)
    place_ref[...] = jnp.zeros_like(place_ref)
    for j in range(n):
        seen_ref[j] = 0
    count = count_ref[0]

    @pl.loop(0, delta_ref.shape[0])
    def _(k):
        c = cols_ref[k]
        j = lax.div(c, per)
        seen = seen_ref[j]
        live = k < count
        fits = jnp.logical_and(live, seen < cap)
        over_ref[k] = jnp.where(jnp.logical_and(live, seen >= cap), 1, 0)

        @pl.when(fits)
        def _():
            pack_ref[j * cap + seen] = delta_ref[k]
            spot = (rows_ref[k] - me * row_blocks) * per + lax.rem(c, per)
            place_ref[j, pl.ds(seen, 1), :] = jnp.full((1, 128), spot, jnp.int32).astype(F32)
            seen_ref[j] = seen + 1


def gather_kernel(
    n, cap, x_ref, gain_ref, wq_hbm, wkv_hbm, pack_ref, place_ref,
    all_ref, q_ref, kv_ref, blocks_ref, places_ref,
    buf, wq, wkv, blocks, places, ss, sr, fs, fr, ws, ds, dr, ms, mr,
):
    me = lax.axis_index("fsdp")
    rows, feats = x_ref.shape
    chips = n // 2
    chip, core = me // 2, me % 2
    load_q = pltpu.make_async_copy(wq_hbm, wq, ws.at[0])
    load_kv = pltpu.make_async_copy(wkv_hbm, wkv, ws.at[1])
    load_q.start()
    load_kv.start()
    buf[me, 0:rows, :] = x_ref[...]
    buf[me, rows : rows + 16, :] = jnp.broadcast_to(
        gain_ref[...].astype(F32), (16, feats)
    ).astype(BF16)
    greet([(me + d) % n for d in range(1, n)])
    sems = (ss, sr, fs, fr)
    out, forwards = spread(n, me, buf, None, 1, sems)
    sent = []
    for d in range(1, n):
        dst = (me + d) % n
        c = rcopy(place_ref.at[dst], places.at[me], ms.at[d], mr.at[d], dst)
        c.start()
        sent.append(c)
        c = rcopy(
            pack_ref.at[pl.ds(dst * cap, cap)], blocks.at[pl.ds(me * cap, cap)], ds.at[d], dr.at[d], dst
        )
        c.start()
        sent.append(c)
    places[me] = place_ref[me]
    for i in range(cap):
        blocks[me * cap + i] = pack_ref[me * cap + i]
    pass_on(n, me, buf, 1, sems, out, forwards)

    def squares(j, total):
        v = buf[j, 0:rows, :].astype(F32)
        return total + jnp.sum(v * v, axis=-1, keepdims=True)

    power = lax.fori_loop(0, n, squares, jnp.zeros((rows, 1), F32)) / (n * feats)
    factor = lax.rsqrt(power + eps)

    def normed(j):
        v = buf[j, 0:rows, :].astype(F32)
        g = buf[j, rows : rows + 16, :].astype(F32)[0:1]
        return (v * factor * g).astype(BF16)

    own = normed(me)
    load_kv.wait()
    kv_ref[...] = jnp.dot(own, wkv[...], preferred_element_type=F32)
    load_q.wait()
    q_ref[...] = jnp.zeros_like(q_ref)

    @pl.loop(0, n)
    def _(j):
        w = wq[pl.ds(pl.multiple_of(j * feats, feats), feats), :]
        v = normed(j)
        for r in range(feats // BLOCK):
            all_ref[j * (feats // BLOCK) + r] = v[:, r * BLOCK : (r + 1) * BLOCK]
        q_ref[...] += jnp.dot(v, w, preferred_element_type=F32)

    for c in sent:
        c.wait()
    blocks_ref[...] = blocks[...]
    places_ref[...] = places[...]


def query_delta_kernel(
    n, split, unroll, cap, rows_ref, cols_ref, over_ref, spot_ref, all_ref, kv_ref, delta_ref,
    q_ref, w_ref, got_ref, msg_ref, query_ref
):
    me = lax.axis_index("fsdp")
    blocks = all_ref.shape[0] // n
    slots = delta_ref.shape[0]
    width = msg_ref.shape[2] - HD
    per = width // BLOCK
    half = kv_ref.shape[1] // 2
    for j in range(n):
        at = (j % 2) * half + (j // split) * HD
        msg_ref[j, :, 0:width] = jnp.zeros((msg_ref.shape[1], width), F32)
        msg_ref[j, :, width : width + HD] = kv_ref[:, at : at + HD]
    query_ref[...] = q_ref[...]
    group = next(u for u in (8, 4, 2, 1) if (n * cap) % u == 0)

    @pl.loop(0, n * cap // group)
    def _(step):
        done = []
        for u in range(group):
            e = step * group + u
            spot = spot_ref[e]
            r = lax.div(e, cap) * blocks + lax.div(spot, per)
            at = pl.ds(pl.multiple_of(lax.rem(spot, per) * BLOCK, BLOCK), BLOCK)
            base = w_ref[pl.ds(pl.multiple_of(r * BLOCK, BLOCK), BLOCK), at]
            merged = (base.astype(F32) + got_ref[e].astype(F32)).astype(BF16)
            lhs = all_ref[r]
            done.append(
                (
                    at,
                    jnp.dot(lhs, merged, preferred_element_type=F32)
                    - jnp.dot(lhs, base, preferred_element_type=F32),
                )
            )
        for at, term in done:
            query_ref[:, at] = query_ref[:, at] + term

    @pl.loop(0, slots // unroll)
    def _(step):
        done = []
        for u in range(unroll):
            k = step * unroll + u
            r = jnp.clip(rows_ref[k] - me * blocks, 0, blocks - 1)
            lhs = all_ref[me * blocks + r]
            lhs = jnp.where(over_ref[k] > 0, lhs, jnp.zeros_like(lhs))
            done.append(jnp.dot(lhs, delta_ref[k], preferred_element_type=F32))
        for u in range(unroll):
            c = cols_ref[step * unroll + u]
            at = pl.ds(pl.multiple_of(lax.rem(c, per) * BLOCK, BLOCK), BLOCK)
            j = lax.div(c, per)
            msg_ref[j, :, at] = msg_ref[j, :, at] + done[u]


def out_delta_kernel(unroll, rows_ref, cols_ref, count_ref, heads_ref, base_ref, delta_ref, out_ref, acc):
    me = lax.axis_index("fsdp")
    slots = delta_ref.shape[0]
    blocks = base_ref.shape[1] // BLOCK
    acc[...] = base_ref[...]
    count = count_ref[0]

    @pl.loop(0, slots // unroll)
    def _(step):
        done = []
        for u in range(unroll):
            k = step * unroll + u
            lhs = heads_ref[rows_ref[k]]
            lhs = jnp.where(k < count, lhs, jnp.zeros_like(lhs))
            done.append(jnp.dot(lhs, delta_ref[k], preferred_element_type=F32))
        for u in range(unroll):
            c = jnp.clip(cols_ref[step * unroll + u] - me * blocks, 0, blocks - 1)
            at = pl.ds(pl.multiple_of(c * BLOCK, BLOCK), BLOCK)
            acc[:, at] = acc[:, at] + done[u]

    out_ref[...] = acc[...].astype(BF16)


def main_kernel(
    n, split, steps, msg, q_ref, cos_ref, sin_ref, len_ref, keys_hbm, values_hbm, wout_hbm,
    heads_out, base_out,
    keys, values, wout, got_a, held_b, got_b, shared, queries, parts, got_parts, mine,
    out_a, out_got_a, out_b, out_got_b, heads,
    ws, as_, ar, bs, br, es, er, ps, pr, oas, oar, obs, obr, ss, sr, fs, fr,
):
    me = lax.axis_index("fsdp")
    chips = n // 2
    chip, core = me // 2, me % 2
    partner = me + 1 - 2 * core
    member = me % split
    first = me - member
    rows, width = q_ref.shape
    per = width // HD
    group = per * split
    seqs = rows // steps
    span = keys.shape[1]
    feats = base_out.shape[1]

    loads = [
        pltpu.make_async_copy(keys_hbm, keys, ws.at[0]),
        pltpu.make_async_copy(values_hbm, values, ws.at[1]),
        pltpu.make_async_copy(wout_hbm, wout, ws.at[2]),
    ]
    for c in loads:
        c.start()
    chip_at = lambda d: (chip + d) % chips
    same = lambda d: 2 * chip_at(d) + core
    mate = lambda e: first + (member + e) % split
    greet([same(d) for d in range(1, chips)] + [mate(e) for e in range(1, split, 2)])

    order = list(range(1, chips)) + [0]
    a = {}
    for d in order:
        a[d] = rcopy(msg.at[2 * chip_at(d) + 1 - core], got_a.at[d], as_.at[d], ar.at[d], partner)
        a[d].start()
    b = {}
    for d in order:
        a[d].wait_recv()
        held_b[d] = msg[2 * chip_at(d) + core] + got_a[d]
        if d:
            b[d] = rcopy(held_b.at[d], got_b.at[d], bs.at[d], br.at[d], same(d))
            b[d].start()
    total = held_b[0]
    for d in range(1, chips):
        b[d].wait_recv()
        total = total + got_b[d]
    cosine, sine = cos_ref[...], sin_ref[...]
    for h in range(per):
        at = slice(h * HD, (h + 1) * HD)
        v = q_ref[:, at] + total[:, at]
        shared[member, :, at] = rope(v, cosine, sine).astype(BF16)
    kv = total[:, width:]
    plain = jnp.broadcast_to(core, kv.shape) == 1
    shared[member, :, width:] = jnp.where(plain, kv, rope(kv, cosine, sine)).astype(BF16)
    ex = []
    for e in range(1, split):
        c = rcopy(shared.at[member], shared.at[member], es.at[e], er.at[e], mate(e))
        c.start()
        ex.append(c)
    for c in ex:
        c.wait_recv()

    for h in range(group):
        at = slice((h % per) * HD, (h % per + 1) * HD)
        queries[h * rows : (h + 1) * rows, :] = shared[h // per, :, at].astype(F32)
    loads[0].wait()
    loads[1].wait()
    scale = HD ** (-0.5)
    spots = member * span + lax.broadcasted_iota(jnp.int32, (group * steps, span), 1)
    for s in range(seqs):
        at = pl.ds(s, group * steps, stride=seqs)
        q = queries[at, :].astype(BF16)
        score = (
            lax.dot_general(q, keys[s], (((1,), (1,)), ((), ())), preferred_element_type=F32)
            * scale
        )
        valid = spots < len_ref[s]
        score = jnp.where(valid, score, masked)
        top = jnp.max(score, axis=-1, keepdims=True)
        weight = jnp.where(valid, jnp.exp(score - top), 0.0)
        shape = (group * steps, HD)
        parts[0, at, :] = jnp.dot(weight.astype(BF16), values[s], preferred_element_type=F32)
        parts[1, at, :] = jnp.broadcast_to(top, shape)
        parts[2, at, :] = jnp.broadcast_to(jnp.sum(weight, axis=-1, keepdims=True), shape)
    chunk = per * rows
    px = []
    for e in range(1, split):
        dst = (member + e) % split
        c = rcopy(
            parts.at[:, pl.ds(dst * chunk, chunk), :], got_parts.at[e], ps.at[e], pr.at[e], mate(e)
        )
        c.start()
        px.append(c)

    new_keys = shared[0, :, width:].astype(F32)
    new_values = shared[1, :, width:].astype(F32)
    step_of = lax.broadcasted_iota(jnp.int32, (rows, 1), 0) // seqs
    fresh = []
    for h in range(per):
        q = shared[member, :, h * HD : (h + 1) * HD].astype(F32)
        scores = []
        for u in range(steps):
            k = jnp.concatenate([new_keys[u * seqs : (u + 1) * seqs]] * steps, axis=0)
            sc = jnp.sum(q * k, axis=-1, keepdims=True) * scale
            scores.append(jnp.where(step_of >= u, sc, masked))
        top = functools.reduce(jnp.maximum, scores)
        tot = jnp.zeros_like(top)
        mix = jnp.zeros((rows, HD), F32)
        for u in range(steps):
            v = jnp.concatenate([new_values[u * seqs : (u + 1) * seqs]] * steps, axis=0)
            w = jnp.where(step_of >= u, jnp.exp(scores[u] - top), 0.0)
            tot = tot + w
            mix = mix + w.astype(BF16).astype(F32) * v
        fresh.append((mix, top, tot))
    for c in px:
        c.wait_recv()
    for h in range(per):
        own = pl.ds(pl.multiple_of(member * chunk + h * rows, rows), rows)
        states = [fresh[h], (parts[0, own, :], parts[1, own, :], parts[2, own, :])]
        for e in range(1, split):
            states.append(tuple(got_parts[e, i, h * rows : (h + 1) * rows, :] for i in range(3)))
        top = functools.reduce(jnp.maximum, [st[1] for st in states])
        mix = jnp.zeros((rows, HD), F32)
        tot = jnp.zeros((rows, HD), F32)
        for st in states:
            w = jnp.exp(st[1] - top)
            mix = mix + st[0] * w
            tot = tot + st[2] * w
        res = (mix / tot).astype(BF16)
        mine[:, h * HD : (h + 1) * HD] = res
        heads[me * per + h] = res

    sems = (ss, sr, fs, fr)
    out, forwards = spread(n, me, heads, None, per, sems)

    loads[2].wait()
    lhs = mine[...]

    def project(dev):
        w = wout[:, pl.ds(pl.multiple_of(dev * feats, feats), feats)]
        return jnp.dot(lhs, w, preferred_element_type=F32)

    oa = {}
    for d in order:
        out_a[d] = project(2 * chip_at(d) + 1 - core)
        oa[d] = rcopy(out_a.at[d], out_got_a.at[d], oas.at[d], oar.at[d], partner)
        oa[d].start()
    ob = {}
    for d in order:
        p = project(same(d))
        oa[d].wait_recv()
        out_b[d] = p + out_got_a[d]
        if d:
            ob[d] = rcopy(out_b.at[d], out_got_b.at[d], obs.at[d], obr.at[d], same(d))
            ob[d].start()
    pass_on(n, me, heads, per, sems, out, forwards)
    heads_out[...] = heads[...]
    total = out_b[0]
    for d in range(1, chips):
        ob[d].wait_recv()
        total = total + out_got_b[d]
    base_out[...] = total
    for c in list(a.values()) + list(b.values()) + ex + px + list(oa.values()) + list(ob.values()):
        c.wait_send()


def dma(k):
    return pltpu.SemaphoreType.DMA((k,))


def local(
    hidden_in, norm_gain, w_query, w_keyval, w_out, q_delta, q_rows, q_cols, q_count,
    o_delta, o_rows, o_cols, o_count, key_cache, value_cache, lengths,
):
    n = lax.axis_size("fsdp")
    chips = n // 2
    steps, seqs, feats = hidden_in.shape
    rows = steps * seqs
    depth, width = w_query.shape
    kv_width = w_keyval.shape[1]
    kvh = kv_width // 2 // HD
    split = n // kvh
    per = width // HD
    group = per * split
    slots = q_delta.shape[0]
    span = key_cache.shape[1]
    msg_width = width + HD
    unroll = next(u for u in (8, 6, 4, 3, 2, 1) if slots % u == 0)

    row_blocks, col_blocks = feats // BLOCK, width // BLOCK
    cap = min(4, row_blocks * col_blocks)
    packed = (n * cap, BLOCK, BLOCK)
    pack, place, over = pl.pallas_call(
        functools.partial(pack_kernel, cap, row_blocks, col_blocks),
        out_shape=(
            jax.ShapeDtypeStruct(packed, BF16),
            jax.ShapeDtypeStruct((n, 8, 128), F32),
            jax.ShapeDtypeStruct((slots,), jnp.int32),
        ),
        in_specs=[SM, SM, SM, VM],
        out_specs=(VM, VM, SM),
        scratch_shapes=[pltpu.SMEM((n,), jnp.int32)],
        compiler_params=pltpu.CompilerParams(vmem_limit_bytes=16 << 20),
        name="pack_query_delta",
    )(q_rows, q_cols, q_count, q_delta)

    normed, query, keyval, blocks, places = pl.pallas_call(
        functools.partial(gather_kernel, n, cap),
        out_shape=(
            jax.ShapeDtypeStruct((n * row_blocks, rows, BLOCK), BF16),
            jax.ShapeDtypeStruct((rows, width), F32),
            jax.ShapeDtypeStruct((rows, kv_width), F32),
            jax.ShapeDtypeStruct(packed, BF16),
            jax.ShapeDtypeStruct((n, 8, 128), F32),
        ),
        in_specs=[VM, VM, ANY, ANY, VM, VM],
        out_specs=(VM, VM, VM, VM, VM),
        scratch_shapes=[
            pltpu.VMEM((n, rows + 16, feats), BF16),
            pltpu.VMEM(w_query.shape, BF16),
            pltpu.VMEM(w_keyval.shape, BF16),
            pltpu.VMEM(packed, BF16),
            pltpu.VMEM((n, 8, 128), F32),
            dma(chips), dma(chips), dma(chips), dma(chips), dma(2),
            dma(n), dma(n), dma(n), dma(n),
        ],
        compiler_params=pltpu.CompilerParams(
            collective_id=0, has_side_effects=True, vmem_limit_bytes=24 << 20
        ),
        name="gather_norm_project",
    )(hidden_in.reshape(rows, feats), norm_gain.reshape(1, feats), w_query, w_keyval, pack, place)
    spots = places[:, :cap, 0].reshape(-1).astype(jnp.int32)

    msg, query = pl.pallas_call(
        functools.partial(query_delta_kernel, n, split, unroll, cap),
        out_shape=(
            jax.ShapeDtypeStruct((n, rows, msg_width), F32),
            jax.ShapeDtypeStruct((rows, width), F32),
        ),
        in_specs=[SM, SM, SM, SM, VM, VM, VM, VM, VM, VM],
        out_specs=(VM, VM),
        compiler_params=pltpu.CompilerParams(vmem_limit_bytes=24 << 20),
        name="query_delta",
    )(q_rows, q_cols, over, spots, normed, keyval, q_delta, query, w_query, blocks)

    position = (lengths[None, :] + jnp.arange(steps, dtype=jnp.int32)[:, None]).astype(F32)
    half = HD // 2
    freq = theta_base ** (-(jnp.arange(half, dtype=F32) * 2.0) / HD)
    angle = position.reshape(rows, 1) * freq
    cosine, sine = jnp.cos(angle), jnp.sin(angle)
    cosine = jnp.concatenate([cosine, cosine], axis=-1)
    sine = jnp.concatenate([-sine, sine], axis=-1)

    vm = pltpu.VMEM
    heads, base = pl.pallas_call(
        functools.partial(main_kernel, n, split, steps),
        out_shape=(
            jax.ShapeDtypeStruct((n * per, rows, HD), BF16),
            jax.ShapeDtypeStruct((rows, feats), F32),
        ),
        in_specs=[VM, VM, VM, VM, SM, ANY, ANY, ANY],
        out_specs=(VM, VM),
        scratch_shapes=[
            vm(key_cache.shape, BF16),
            vm(value_cache.shape, BF16),
            vm(w_out.shape, BF16),
            vm((chips, rows, msg_width), F32),
            vm((chips, rows, msg_width), F32),
            vm((chips, rows, msg_width), F32),
            vm((split, rows, msg_width), BF16),
            vm((group * rows, HD), F32),
            vm((3, group * rows, HD), F32),
            vm((split, 3, per * rows, HD), F32),
            vm((rows, width), BF16),
            vm((chips, rows, feats), F32),
            vm((chips, rows, feats), F32),
            vm((chips, rows, feats), F32),
            vm((chips, rows, feats), F32),
            vm((n * per, rows, HD), BF16),
            dma(3),
            dma(chips), dma(chips), dma(chips), dma(chips),
            dma(split), dma(split), dma(split), dma(split),
            dma(chips), dma(chips), dma(chips), dma(chips),
            dma(chips), dma(chips), dma(chips), dma(chips),
        ],
        compiler_params=pltpu.CompilerParams(
            collective_id=1, has_side_effects=True, vmem_limit_bytes=40 << 20
        ),
        name="attend_project",
    )(msg, query, cosine, sine, lengths, key_cache, value_cache, w_out)

    out = pl.pallas_call(
        functools.partial(out_delta_kernel, unroll),
        out_shape=jax.ShapeDtypeStruct((rows, feats), BF16),
        in_specs=[SM, SM, SM, VM, VM, VM],
        out_specs=VM,
        scratch_shapes=[vm((rows, feats), F32)],
        compiler_params=pltpu.CompilerParams(vmem_limit_bytes=24 << 20),
        name="out_delta",
    )(o_rows, o_cols, o_count, heads, base, o_delta)
    return out.reshape(steps, seqs, feats)


def solution(mesh):
    both = ("groups", "fsdp")
    in_specs = (
        P(None, "groups", "fsdp"),
        P("fsdp"),
        P(None, "fsdp"),
        P("fsdp", None),
        P("fsdp", None),
        P(both, None, None),
        P(both),
        P(both),
        P(both),
        P(both, None, None),
        P(both),
        P(both),
        P(both),
        P("groups", "fsdp", None),
        P("groups", "fsdp", None),
        P("groups"),
    )
    out_specs = P(None, "groups", "fsdp")
    return jax.shard_map(local, mesh=mesh, in_specs=in_specs, out_specs=out_specs, check_vma=False)
```

```python
import functools

import jax
import jax.numpy as jnp
from jax import lax
from jax.experimental import pallas as pl
from jax.experimental.pallas import tpu as pltpu
from jax.sharding import PartitionSpec as P

HD = 128
BLOCK = 128
theta_base = 1000000.0
eps = 1e-06
masked = -1e30
MESH = pl.DeviceIdType.MESH
F32 = jnp.float32
BF16 = jnp.bfloat16
VM = pl.BlockSpec(memory_space=pltpu.VMEM)
SM = pl.BlockSpec(memory_space=pltpu.SMEM)
ANY = pl.BlockSpec(memory_space=pl.ANY)


def rcopy(src, dst, send, recv, device):
    return pltpu.make_async_remote_copy(
        src_ref=src, dst_ref=dst, send_sem=send, recv_sem=recv,
        device_id={"fsdp": device}, device_id_type=MESH,
    )


def greet(devices):
    barrier = pltpu.get_barrier_semaphore()
    for device in devices:
        pl.semaphore_signal(barrier, inc=1, device_id={"fsdp": device}, device_id_type=MESH)
    pl.semaphore_wait(barrier, len(devices))


def spread(n, me, buf, start, size, sems):
    chips = n // 2
    chip, core = me // 2, me % 2
    partner = me + 1 - 2 * core
    ss, sr, fs, fr = sems
    view = lambda dev: buf.at[pl.ds(dev * size, size)]
    out = []
    for d in range(1, chips):
        dst = 2 * ((chip + d) % chips) + core
        c = rcopy(view(me), view(me), ss.at[d], sr.at[d], dst)
        c.start()
        out.append(c)
    c = rcopy(view(me), view(me), fs.at[0], fr.at[0], partner)
    c.start()
    forwards = [c]
    return out, forwards


def pass_on(n, me, buf, size, sems, out, forwards):
    chips = n // 2
    chip, core = me // 2, me % 2
    partner = me + 1 - 2 * core
    ss, sr, fs, fr = sems
    for d in range(1, chips):
        out[d - 1].wait_recv()
        src = 2 * ((chip + chips - d) % chips) + core
        v = buf.at[pl.ds(src * size, size)]
        c = rcopy(v, v, fs.at[d], fr.at[d], partner)
        c.start()
        forwards.append(c)
    for c in forwards:
        c.wait_recv()
    for c in out + forwards:
        c.wait_send()


def rope(v, cosine, sine):
    return v * cosine + pltpu.roll(v, HD // 2, 1) * sine


def pack_kernel(
    cap, row_blocks, per, rows_ref, cols_ref, count_ref, delta_ref, pack_ref, place_ref, over_ref, seen_ref
):
    me = lax.axis_index("fsdp")
    n = place_ref.shape[0]
    pack_ref[...] = jnp.zeros_like(pack_ref)
    place_ref[...] = jnp.zeros_like(place_ref)
    for j in range(n):
        seen_ref[j] = 0
    count = count_ref[0]

    @pl.loop(0, delta_ref.shape[0])
    def _(k):
        c = cols_ref[k]
        j = lax.div(c, per)
        seen = seen_ref[j]
        live = k < count
        fits = jnp.logical_and(live, seen < cap)
        over_ref[k] = jnp.where(jnp.logical_and(live, seen >= cap), 1, 0)

        @pl.when(fits)
        def _():
            pack_ref[j * cap + seen] = delta_ref[k]
            spot = (rows_ref[k] - me * row_blocks) * per + lax.rem(c, per)
            place_ref[j, pl.ds(seen, 1), :] = jnp.full((1, 128), spot, jnp.int32).astype(F32)
            seen_ref[j] = seen + 1


def gather_kernel(
    n, cap, x_ref, gain_ref, wq_hbm, wkv_hbm, pack_ref, place_ref,
    all_ref, q_ref, kv_ref, blocks_ref, places_ref,
    buf, wq, wkv, blocks, places, ss, sr, fs, fr, ws, ds, dr, ms, mr,
):
    me = lax.axis_index("fsdp")
    rows, feats = x_ref.shape
    chips = n // 2
    chip, core = me // 2, me % 2
    load_q = pltpu.make_async_copy(wq_hbm, wq, ws.at[0])
    load_kv = pltpu.make_async_copy(wkv_hbm, wkv, ws.at[1])
    load_q.start()
    load_kv.start()
    buf[me, 0:rows, :] = x_ref[...]
    buf[me, rows : rows + 16, :] = jnp.broadcast_to(
        gain_ref[...].astype(F32), (16, feats)
    ).astype(BF16)
    greet([(me + d) % n for d in range(1, n)])
    sems = (ss, sr, fs, fr)
    out, forwards = spread(n, me, buf, None, 1, sems)
    sent = []
    for d in range(1, n):
        dst = (me + d) % n
        c = rcopy(place_ref.at[dst], places.at[me], ms.at[d], mr.at[d], dst)
        c.start()
        sent.append(c)
        c = rcopy(
            pack_ref.at[pl.ds(dst * cap, cap)], blocks.at[pl.ds(me * cap, cap)], ds.at[d], dr.at[d], dst
        )
        c.start()
        sent.append(c)
    places[me] = place_ref[me]
    for i in range(cap):
        blocks[me * cap + i] = pack_ref[me * cap + i]
    pass_on(n, me, buf, 1, sems, out, forwards)

    def squares(j, total):
        v = buf[j, 0:rows, :].astype(F32)
        return total + jnp.sum(v * v, axis=-1, keepdims=True)

    power = lax.fori_loop(0, n, squares, jnp.zeros((rows, 1), F32)) / (n * feats)
    factor = lax.rsqrt(power + eps)

    def normed(j):
        v = buf[j, 0:rows, :].astype(F32)
        g = buf[j, rows : rows + 16, :].astype(F32)[0:1]
        return (v * factor * g).astype(BF16)

    own = normed(me)
    load_kv.wait()
    kv_ref[...] = jnp.dot(own, wkv[...], preferred_element_type=F32)
    load_q.wait()
    q_ref[...] = jnp.zeros_like(q_ref)

    @pl.loop(0, n)
    def _(j):
        w = wq[pl.ds(pl.multiple_of(j * feats, feats), feats), :]
        v = normed(j)
        for r in range(feats // BLOCK):
            all_ref[j * (feats // BLOCK) + r] = v[:, r * BLOCK : (r + 1) * BLOCK]
        q_ref[...] += jnp.dot(v, w, preferred_element_type=F32)

    for c in sent:
        c.wait()
    blocks_ref[...] = blocks[...]
    places_ref[...] = places[...]


def query_delta_kernel(
    n, split, unroll, cap, rows_ref, cols_ref, over_ref, spot_ref, all_ref, kv_ref, delta_ref,
    q_ref, w_hbm, got_ref, msg_ref, query_ref, w_ref, load_sem
):
    me = lax.axis_index("fsdp")
    load = pltpu.make_async_copy(w_hbm, w_ref, load_sem.at[0])
    load.start()
    blocks = all_ref.shape[0] // n
    slots = delta_ref.shape[0]
    width = msg_ref.shape[2] - HD
    per = width // BLOCK
    half = kv_ref.shape[1] // 2
    for j in range(n):
        at = (j % 2) * half + (j // split) * HD
        msg_ref[j, :, 0:width] = jnp.zeros((msg_ref.shape[1], width), F32)
        msg_ref[j, :, width : width + HD] = kv_ref[:, at : at + HD]
    @pl.loop(0, slots // unroll)
    def _(step):
        done = []
        for u in range(unroll):
            k = step * unroll + u
            r = jnp.clip(rows_ref[k] - me * blocks, 0, blocks - 1)
            lhs = all_ref[me * blocks + r]
            lhs = jnp.where(over_ref[k] > 0, lhs, jnp.zeros_like(lhs))
            done.append(jnp.dot(lhs, delta_ref[k], preferred_element_type=F32))
        for u in range(unroll):
            c = cols_ref[step * unroll + u]
            at = pl.ds(pl.multiple_of(lax.rem(c, per) * BLOCK, BLOCK), BLOCK)
            j = lax.div(c, per)
            msg_ref[j, :, at] = msg_ref[j, :, at] + done[u]

    query_ref[...] = q_ref[...]
    load.wait()
    group = next(u for u in (8, 4, 2, 1) if (n * cap) % u == 0)

    @pl.loop(0, n * cap // group)
    def _(step):
        done = []
        for u in range(group):
            e = step * group + u
            spot = spot_ref[e]
            r = lax.div(e, cap) * blocks + lax.div(spot, per)
            at = pl.ds(pl.multiple_of(lax.rem(spot, per) * BLOCK, BLOCK), BLOCK)
            base = w_ref[pl.ds(pl.multiple_of(r * BLOCK, BLOCK), BLOCK), at]
            merged = (base.astype(F32) + got_ref[e].astype(F32)).astype(BF16)
            lhs = all_ref[r]
            done.append(
                (
                    at,
                    jnp.dot(lhs, merged, preferred_element_type=F32)
                    - jnp.dot(lhs, base, preferred_element_type=F32),
                )
            )
        for at, term in done:
            query_ref[:, at] = query_ref[:, at] + term


def out_delta_kernel(unroll, rows_ref, cols_ref, count_ref, heads_ref, base_ref, delta_ref, out_ref, acc):
    me = lax.axis_index("fsdp")
    slots = delta_ref.shape[0]
    blocks = base_ref.shape[1] // BLOCK
    acc[...] = base_ref[...]
    count = count_ref[0]

    @pl.loop(0, slots // unroll)
    def _(step):
        done = []
        for u in range(unroll):
            k = step * unroll + u
            lhs = heads_ref[rows_ref[k]]
            lhs = jnp.where(k < count, lhs, jnp.zeros_like(lhs))
            done.append(jnp.dot(lhs, delta_ref[k], preferred_element_type=F32))
        for u in range(unroll):
            c = jnp.clip(cols_ref[step * unroll + u] - me * blocks, 0, blocks - 1)
            at = pl.ds(pl.multiple_of(c * BLOCK, BLOCK), BLOCK)
            acc[:, at] = acc[:, at] + done[u]

    out_ref[...] = acc[...].astype(BF16)


def main_kernel(
    n, split, steps, msg, q_ref, cos_ref, sin_ref, len_ref, keys_hbm, values_hbm, wout_hbm,
    heads_out, base_out,
    keys, values, wout, got_a, held_b, got_b, shared, queries, parts, got_parts, mine,
    out_a, out_got_a, out_b, out_got_b, heads,
    ws, as_, ar, bs, br, es, er, ps, pr, oas, oar, obs, obr, ss, sr, fs, fr,
):
    me = lax.axis_index("fsdp")
    chips = n // 2
    chip, core = me // 2, me % 2
    partner = me + 1 - 2 * core
    member = me % split
    first = me - member
    rows, width = q_ref.shape
    per = width // HD
    group = per * split
    seqs = rows // steps
    span = keys.shape[1]
    feats = base_out.shape[1]

    loads = [
        pltpu.make_async_copy(keys_hbm, keys, ws.at[0]),
        pltpu.make_async_copy(values_hbm, values, ws.at[1]),
        pltpu.make_async_copy(wout_hbm, wout, ws.at[2]),
    ]
    for c in loads:
        c.start()
    chip_at = lambda d: (chip + d) % chips
    same = lambda d: 2 * chip_at(d) + core
    mate = lambda e: first + (member + e) % split
    greet([same(d) for d in range(1, chips)] + [mate(e) for e in range(1, split, 2)])

    order = list(range(1, chips)) + [0]
    a = {}
    for d in order:
        a[d] = rcopy(msg.at[2 * chip_at(d) + 1 - core], got_a.at[d], as_.at[d], ar.at[d], partner)
        a[d].start()
    b = {}
    for d in order:
        a[d].wait_recv()
        held_b[d] = msg[2 * chip_at(d) + core] + got_a[d]
        if d:
            b[d] = rcopy(held_b.at[d], got_b.at[d], bs.at[d], br.at[d], same(d))
            b[d].start()
    total = held_b[0]
    for d in range(1, chips):
        b[d].wait_recv()
        total = total + got_b[d]
    cosine, sine = cos_ref[...], sin_ref[...]
    for h in range(per):
        at = slice(h * HD, (h + 1) * HD)
        v = q_ref[:, at] + total[:, at]
        shared[member, :, at] = rope(v, cosine, sine).astype(BF16)
    kv = total[:, width:]
    plain = jnp.broadcast_to(core, kv.shape) == 1
    shared[member, :, width:] = jnp.where(plain, kv, rope(kv, cosine, sine)).astype(BF16)
    ex = []
    for e in range(1, split):
        c = rcopy(shared.at[member], shared.at[member], es.at[e], er.at[e], mate(e))
        c.start()
        ex.append(c)
    for c in ex:
        c.wait_recv()

    for h in range(group):
        at = slice((h % per) * HD, (h % per + 1) * HD)
        queries[h * rows : (h + 1) * rows, :] = shared[h // per, :, at].astype(F32)
    loads[0].wait()
    loads[1].wait()
    scale = HD ** (-0.5)
    spots = member * span + lax.broadcasted_iota(jnp.int32, (group * steps, span), 1)
    for s in range(seqs):
        at = pl.ds(s, group * steps, stride=seqs)
        q = queries[at, :].astype(BF16)
        score = (
            lax.dot_general(q, keys[s], (((1,), (1,)), ((), ())), preferred_element_type=F32)
            * scale
        )
        valid = spots < len_ref[s]
        score = jnp.where(valid, score, masked)
        top = jnp.max(score, axis=-1, keepdims=True)
        weight = jnp.where(valid, jnp.exp(score - top), 0.0)
        shape = (group * steps, HD)
        parts[0, at, :] = jnp.dot(weight.astype(BF16), values[s], preferred_element_type=F32)
        parts[1, at, :] = jnp.broadcast_to(top, shape)
        parts[2, at, :] = jnp.broadcast_to(jnp.sum(weight, axis=-1, keepdims=True), shape)
    chunk = per * rows
    px = []
    for e in range(1, split):
        dst = (member + e) % split
        c = rcopy(
            parts.at[:, pl.ds(dst * chunk, chunk), :], got_parts.at[e], ps.at[e], pr.at[e], mate(e)
        )
        c.start()
        px.append(c)

    new_keys = shared[0, :, width:].astype(F32)
    new_values = shared[1, :, width:].astype(F32)
    step_of = lax.broadcasted_iota(jnp.int32, (rows, 1), 0) // seqs
    fresh = []
    for h in range(per):
        q = shared[member, :, h * HD : (h + 1) * HD].astype(F32)
        scores = []
        for u in range(steps):
            k = jnp.concatenate([new_keys[u * seqs : (u + 1) * seqs]] * steps, axis=0)
            sc = jnp.sum(q * k, axis=-1, keepdims=True) * scale
            scores.append(jnp.where(step_of >= u, sc, masked))
        top = functools.reduce(jnp.maximum, scores)
        tot = jnp.zeros_like(top)
        mix = jnp.zeros((rows, HD), F32)
        for u in range(steps):
            v = jnp.concatenate([new_values[u * seqs : (u + 1) * seqs]] * steps, axis=0)
            w = jnp.where(step_of >= u, jnp.exp(scores[u] - top), 0.0)
            tot = tot + w
            mix = mix + w.astype(BF16).astype(F32) * v
        fresh.append((mix, top, tot))
    for c in px:
        c.wait_recv()
    for h in range(per):
        own = pl.ds(pl.multiple_of(member * chunk + h * rows, rows), rows)
        states = [fresh[h], (parts[0, own, :], parts[1, own, :], parts[2, own, :])]
        for e in range(1, split):
            states.append(tuple(got_parts[e, i, h * rows : (h + 1) * rows, :] for i in range(3)))
        top = functools.reduce(jnp.maximum, [st[1] for st in states])
        mix = jnp.zeros((rows, HD), F32)
        tot = jnp.zeros((rows, HD), F32)
        for st in states:
            w = jnp.exp(st[1] - top)
            mix = mix + st[0] * w
            tot = tot + st[2] * w
        res = (mix / tot).astype(BF16)
        mine[:, h * HD : (h + 1) * HD] = res
        heads[me * per + h] = res

    sems = (ss, sr, fs, fr)
    out, forwards = spread(n, me, heads, None, per, sems)

    loads[2].wait()
    lhs = mine[...]

    def project(dev):
        w = wout[:, pl.ds(pl.multiple_of(dev * feats, feats), feats)]
        return jnp.dot(lhs, w, preferred_element_type=F32)

    oa = {}
    for d in order:
        out_a[d] = project(2 * chip_at(d) + 1 - core)
        oa[d] = rcopy(out_a.at[d], out_got_a.at[d], oas.at[d], oar.at[d], partner)
        oa[d].start()
    ob = {}
    for d in order:
        p = project(same(d))
        oa[d].wait_recv()
        out_b[d] = p + out_got_a[d]
        if d:
            ob[d] = rcopy(out_b.at[d], out_got_b.at[d], obs.at[d], obr.at[d], same(d))
            ob[d].start()
    pass_on(n, me, heads, per, sems, out, forwards)
    heads_out[...] = heads[...]
    total = out_b[0]
    for d in range(1, chips):
        ob[d].wait_recv()
        total = total + out_got_b[d]
    base_out[...] = total
    for c in list(a.values()) + list(b.values()) + ex + px + list(oa.values()) + list(ob.values()):
        c.wait_send()


def dma(k):
    return pltpu.SemaphoreType.DMA((k,))


def local(
    hidden_in, norm_gain, w_query, w_keyval, w_out, q_delta, q_rows, q_cols, q_count,
    o_delta, o_rows, o_cols, o_count, key_cache, value_cache, lengths,
):
    n = lax.axis_size("fsdp")
    chips = n // 2
    steps, seqs, feats = hidden_in.shape
    rows = steps * seqs
    depth, width = w_query.shape
    kv_width = w_keyval.shape[1]
    kvh = kv_width // 2 // HD
    split = n // kvh
    per = width // HD
    group = per * split
    slots = q_delta.shape[0]
    span = key_cache.shape[1]
    msg_width = width + HD
    unroll = next(u for u in (8, 6, 4, 3, 2, 1) if slots % u == 0)

    row_blocks, col_blocks = feats // BLOCK, width // BLOCK
    cap = min(4, row_blocks * col_blocks)
    packed = (n * cap, BLOCK, BLOCK)
    pack, place, over = pl.pallas_call(
        functools.partial(pack_kernel, cap, row_blocks, col_blocks),
        out_shape=(
            jax.ShapeDtypeStruct(packed, BF16),
            jax.ShapeDtypeStruct((n, 8, 128), F32),
            jax.ShapeDtypeStruct((slots,), jnp.int32),
        ),
        in_specs=[SM, SM, SM, VM],
        out_specs=(VM, VM, SM),
        scratch_shapes=[pltpu.SMEM((n,), jnp.int32)],
        compiler_params=pltpu.CompilerParams(vmem_limit_bytes=16 << 20),
        name="pack_query_delta",
    )(q_rows, q_cols, q_count, q_delta)

    normed, query, keyval, blocks, places = pl.pallas_call(
        functools.partial(gather_kernel, n, cap),
        out_shape=(
            jax.ShapeDtypeStruct((n * row_blocks, rows, BLOCK), BF16),
            jax.ShapeDtypeStruct((rows, width), F32),
            jax.ShapeDtypeStruct((rows, kv_width), F32),
            jax.ShapeDtypeStruct(packed, BF16),
            jax.ShapeDtypeStruct((n, 8, 128), F32),
        ),
        in_specs=[VM, VM, ANY, ANY, VM, VM],
        out_specs=(VM, VM, VM, VM, VM),
        scratch_shapes=[
            pltpu.VMEM((n, rows + 16, feats), BF16),
            pltpu.VMEM(w_query.shape, BF16),
            pltpu.VMEM(w_keyval.shape, BF16),
            pltpu.VMEM(packed, BF16),
            pltpu.VMEM((n, 8, 128), F32),
            dma(chips), dma(chips), dma(chips), dma(chips), dma(2),
            dma(n), dma(n), dma(n), dma(n),
        ],
        compiler_params=pltpu.CompilerParams(
            collective_id=0, has_side_effects=True, vmem_limit_bytes=54 << 20
        ),
        name="gather_norm_project",
    )(hidden_in.reshape(rows, feats), norm_gain.reshape(1, feats), w_query, w_keyval, pack, place)
    spots = places[:, :cap, 0].reshape(-1).astype(jnp.int32)

    msg, query = pl.pallas_call(
        functools.partial(query_delta_kernel, n, split, unroll, cap),
        out_shape=(
            jax.ShapeDtypeStruct((n, rows, msg_width), F32),
            jax.ShapeDtypeStruct((rows, width), F32),
        ),
        in_specs=[SM, SM, SM, SM, VM, VM, VM, VM, ANY, VM],
        out_specs=(VM, VM),
        scratch_shapes=[pltpu.VMEM(w_query.shape, BF16), dma(1)],
        compiler_params=pltpu.CompilerParams(vmem_limit_bytes=52 << 20),
        name="query_delta",
    )(q_rows, q_cols, over, spots, normed, keyval, q_delta, query, w_query, blocks)

    position = (lengths[None, :] + jnp.arange(steps, dtype=jnp.int32)[:, None]).astype(F32)
    half = HD // 2
    freq = theta_base ** (-(jnp.arange(half, dtype=F32) * 2.0) / HD)
    angle = position.reshape(rows, 1) * freq
    cosine, sine = jnp.cos(angle), jnp.sin(angle)
    cosine = jnp.concatenate([cosine, cosine], axis=-1)
    sine = jnp.concatenate([-sine, sine], axis=-1)

    vm = pltpu.VMEM
    heads, base = pl.pallas_call(
        functools.partial(main_kernel, n, split, steps),
        out_shape=(
            jax.ShapeDtypeStruct((n * per, rows, HD), BF16),
            jax.ShapeDtypeStruct((rows, feats), F32),
        ),
        in_specs=[VM, VM, VM, VM, SM, ANY, ANY, ANY],
        out_specs=(VM, VM),
        scratch_shapes=[
            vm(key_cache.shape, BF16),
            vm(value_cache.shape, BF16),
            vm(w_out.shape, BF16),
            vm((chips, rows, msg_width), F32),
            vm((chips, rows, msg_width), F32),
            vm((chips, rows, msg_width), F32),
            vm((split, rows, msg_width), BF16),
            vm((group * rows, HD), F32),
            vm((3, group * rows, HD), F32),
            vm((split, 3, per * rows, HD), F32),
            vm((rows, width), BF16),
            vm((chips, rows, feats), F32),
            vm((chips, rows, feats), F32),
            vm((chips, rows, feats), F32),
            vm((chips, rows, feats), F32),
            vm((n * per, rows, HD), BF16),
            dma(3),
            dma(chips), dma(chips), dma(chips), dma(chips),
            dma(split), dma(split), dma(split), dma(split),
            dma(chips), dma(chips), dma(chips), dma(chips),
            dma(chips), dma(chips), dma(chips), dma(chips),
        ],
        compiler_params=pltpu.CompilerParams(
            collective_id=1, has_side_effects=True, vmem_limit_bytes=57 << 20
        ),
        name="attend_project",
    )(msg, query, cosine, sine, lengths, key_cache, value_cache, w_out)

    out = pl.pallas_call(
        functools.partial(out_delta_kernel, unroll),
        out_shape=jax.ShapeDtypeStruct((rows, feats), BF16),
        in_specs=[SM, SM, SM, VM, VM, VM],
        out_specs=VM,
        scratch_shapes=[vm((rows, feats), F32)],
        compiler_params=pltpu.CompilerParams(vmem_limit_bytes=24 << 20),
        name="out_delta",
    )(o_rows, o_cols, o_count, heads, base, o_delta)
    return out.reshape(steps, seqs, feats)


def solution(mesh):
    both = ("groups", "fsdp")
    in_specs = (
        P(None, "groups", "fsdp"),
        P("fsdp"),
        P(None, "fsdp"),
        P("fsdp", None),
        P("fsdp", None),
        P(both, None, None),
        P(both),
        P(both),
        P(both),
        P(both, None, None),
        P(both),
        P(both),
        P(both),
        P("groups", "fsdp", None),
        P("groups", "fsdp", None),
        P("groups"),
    )
    out_specs = P(None, "groups", "fsdp")
    return jax.shard_map(local, mesh=mesh, in_specs=in_specs, out_specs=out_specs, check_vma=False)
```
